32 devices in a mesh: groups: 2 (over x), slab: 8 (over z, y), sub: 2 (over core).
Axes of the slice: x: 2, y: 2, z: 4, core: 2. Of those that a mesh axis runs over, the one named last changes fastest.
Arguments:
- features: float32 [128, 64, 512], P(('groups', 'slab'), 'sub'), parts along dimension 0, may hold values from -6 to 6
- block_count: int32 [16], P(('groups', 'slab')), parts along dimension 0, may hold values from 4 to 8, as said below
- neighbours: int32 [128, 27], P(('groups', 'slab')), parts along dimension 0, may hold values from 0 to 24, as said below
- conv_weight: float32 [27, 64, 64], P(None, 'sub'), may hold values from -0.15625 to 0.15625
- lift_weight: float32 [128, 64], replicated, may hold values from -0.75 to 0.75
- drop_weight: float32 [64, 128], P('sub'), may hold values from -0.5 to 0.5
- cotangent: float32 [128, 64, 512], P(('groups', 'slab'), 'sub'), parts along dimension 0, may hold values from -6 to 6
Outputs:
- output: float32 [128, 64, 512], P(('groups', 'slab'), 'sub'), parts along dimension 0
- feature_grad: float32 [128, 64, 512], P(('groups', 'slab'), 'sub'), parts along dimension 0
- weight_grad: float32 [27, 128, 64], P(None, ('groups', 'sub')), parts along dimension 1
The draws below stay inside these ranges and needn't reach their ends.
There are 2 independent parts, one for each index of `groups`. The reference program is written for one: setup_inputs(seed, part) draws one part's arguments, and reference() takes and returns one part's arrays. A program takes and returns all parts, laid end to end along the dimension named above; an argument that names none is the same for every part. Nothing has to cross between parts.
Inputs may be any that keep to these rules, and one draw needn't show every extreme that they name: `block_count`: each slab has between 4 and 8 live slots, the live ones first; some slab has all 8 live. `neighbours`: entries are 3 * 8 (no neighbour) or a slot of slab s-1 (0 .. 7), s (8 .. 15) or s+1 (16 .. 23) of the table; the centre offset 13 is the block itself. Slabs at the ends name no slab beyond them.
All inputs are finite; a program needn't handle non-finite values.
Results may differ from the reference program's by a relative error of at most 0.00008.
Values sent between devices are 32-bit elements; how exact they have to be, the bound alone decides.
A program may use at most 128 MiB of HBM per device.

```python
import jax
import jax.numpy as jnp
from jax import lax

C = 64
HID = 128
NB = 8
NBLK = 64
N_SLAB = 8


def shared_counts(key):
    base = jax.random.fold_in(key, 101)
    counts = jax.random.randint(base, (N_SLAB,), NB // 2, NB + 1)
    top = jax.random.randint(jax.random.fold_in(base, 1), (), 0, N_SLAB)
    return counts.at[top].set(NB).astype(jnp.int32)


def draw_block_count(key, part):
    return shared_counts(key)


def draw_neighbours(key, part):
    counts = shared_counts(key)
    key = jax.random.fold_in(key, 7)
    rows = jnp.arange(NBLK, dtype=jnp.int32)
    slabs = rows // NB
    slots = rows % NB
    offsets = jnp.arange(27, dtype=jnp.int32) // 9 - 1
    moved = (slots % 2)[:, None] + offsets[None, :]
    side = jnp.floor_divide(moved, 2)
    target = slabs[:, None] + side
    valid = (target >= 0) & (target < N_SLAB)
    avail = counts[jnp.clip(target, 0, N_SLAB - 1)]
    picks = jax.random.randint(jax.random.fold_in(key, 1), (NBLK, 27), 0, 1 << 20) % avail
    empty = jax.random.randint(jax.random.fold_in(key, 2), (NBLK, 27), 0, 4) == 0
    index = jnp.where(valid & jnp.logical_not(empty), (side + 1) * NB + picks, 3 * NB)
    index = index.at[:, 13].set(NB + slots)
    return index.astype(jnp.int32)


def levels(rng, shape, cuts, smallest, top_value):
    gain = 1.0
    for axis_at, blocks in cuts:
        draws = jax.random.uniform(jax.random.fold_in(jax.random.fold_in(rng, 6), axis_at), (blocks,), jnp.float32, smallest / len(cuts), top_value / len(cuts))
        gain = gain * jnp.repeat(jnp.exp(draws), shape[axis_at] // blocks).reshape((-1,) + (1,) * (len(shape) - 1 - axis_at))
    return gain


def normal_values(own_key, shape, deviation, limit, cuts=(), kind=jnp.bfloat16):
    array = deviation * jax.random.normal(own_key, shape, jnp.float32)
    if cuts:
        array = array * levels(own_key, shape, cuts, -0.22, 0.18)
    return jnp.clip(array, -limit, limit).astype(kind)


def setup_inputs(seed: int = 0, part: int = 0) -> dict:
    streams_of = jax.random.split(jax.random.key(seed), 8)
    own_keys = jax.random.split(jax.random.fold_in(streams_of[7], part), 8)
    features = normal_values(own_keys[0], (NBLK, C, 512), 1.0, 6.0, ((0, 8), (1, 2)), jnp.float32)
    block_count = draw_block_count(jax.random.fold_in(jax.random.fold_in(streams_of[7], part), 71), part)
    neighbours = draw_neighbours(jax.random.fold_in(jax.random.fold_in(streams_of[7], part), 71), part)
    conv_weight = normal_values(streams_of[3], (27, C, C), (27 * C) ** -0.5, 0.15625, ((1, 2),), jnp.float32)
    lift_weight = normal_values(streams_of[4], (HID, C), C ** -0.5, 0.75, (), jnp.float32)
    drop_weight = normal_values(streams_of[5], (C, HID), HID ** -0.5, 0.5, ((0, 2),), jnp.float32)
    cotangent = normal_values(own_keys[6], (NBLK, C, 512), 1.0, 6.0, ((0, 8), (1, 2)), jnp.float32)
    return dict(features=features, block_count=block_count, neighbours=neighbours, conv_weight=conv_weight, lift_weight=lift_weight, drop_weight=drop_weight, cotangent=cotangent)


HIGH = lax.Precision.HIGHEST

def assemble(near):
    first = jnp.concatenate([near[0][..., 7:8, :, :], near[1], near[2][..., 0:1, :, :]], axis=-3)
    second = jnp.concatenate([first[0][..., 7:8, :], first[1], first[2][..., 0:1, :]], axis=-2)
    return jnp.concatenate([second[0][..., 7:8], second[1], second[2][..., 0:1]], axis=-1)

def conv_blocks(table, rows, weight):
    chans = table.shape[1]

    def single(row):
        near = table[row].reshape(3, 3, 3, chans, 8, 8, 8)
        patch = assemble(near)
        cols = jnp.stack([patch[:, a:a + 8, b:b + 8, c:c + 8].reshape(chans, 512) for a in range(3) for b in range(3) for c in range(3)])
        return jnp.einsum('koi,kiv->ov', weight, cols, precision=HIGH)
    return lax.map(jax.checkpoint(single), rows)

def pool_blocks(fine):
    count, chans, _ = fine.shape
    view = fine.reshape(count // 8, 2, 2, 2, chans, 4, 2, 4, 2, 4, 2).mean(axis=(6, 8, 10))
    return view.transpose(0, 4, 1, 5, 2, 6, 3, 7).reshape(count // 8, chans, 512)

def spread_blocks(coarse):
    count, chans, _ = coarse.shape
    view = coarse.reshape(count, chans, 2, 4, 2, 4, 2, 4).transpose(0, 2, 4, 6, 1, 3, 5, 7)
    view = jnp.broadcast_to(view[..., :, None, :, None, :, None], (count, 2, 2, 2, chans, 4, 2, 4, 2, 4, 2))
    return view.reshape(count * 8, chans, 512)

def reference(features, block_count, neighbours, conv_weight, lift_weight, drop_weight, cotangent):
    rows = jnp.arange(NBLK, dtype=jnp.int32)
    slabs = rows // NB
    live = (rows % NB < block_count[slabs]).astype(features.dtype)[:, None, None]
    global_rows = jnp.where(neighbours == 3 * NB, NBLK + 2 * NB, slabs[:, None] * NB + neighbours).astype(jnp.int32)

    def forward(feat, weight):
        chans = feat.shape[1]
        table = jnp.concatenate([jnp.zeros((NB, chans, 512), feat.dtype), feat, jnp.zeros((NB + 1, chans, 512), feat.dtype)], axis=0)
        pre = conv_blocks(table, global_rows, weight)
        hidden = jax.nn.silu(pre)
        pooled = pool_blocks(hidden * live)
        lifted = jax.nn.silu(jnp.einsum('hc,ncv->nhv', lift_weight, pooled, precision=HIGH))
        coarse = jnp.einsum('ch,nhv->ncv', drop_weight, lifted, precision=HIGH)
        return live * (hidden + spread_blocks(coarse))
    output, pull = jax.vjp(forward, features, conv_weight)
    feature_grad, grad = pull(cotangent)
    weight_grad = grad / jnp.sqrt(jnp.float32(512 * NBLK)).astype(grad.dtype)
    return (output, feature_grad, weight_grad)
```

```python
import functools

import jax
import jax.numpy as jnp
from jax import lax
from jax.experimental import pallas as pl
from jax.experimental.pallas import tpu as pltpu
from jax.sharding import PartitionSpec as P

HIGH = lax.Precision.HIGHEST
F32 = jnp.float32
BF16 = jnp.bfloat16
K = 27
VOX = 512
LANES = 128
CH = 16
PIECES = VOX // LANES


def split(x):
    hi = x.astype(BF16)
    lo = (x - hi.astype(F32)).astype(BF16)
    return hi, lo


def dot(a, b):
    return jnp.dot(a, b, preferred_element_type=F32)


def dot_nt(a, b):
    return lax.dot_general(a, b, (((1,), (1,)), ((), ())), preferred_element_type=F32)


def rolled(x, by):
    return pltpu.roll(x, by % LANES, axis=1)


def gather_patch(nb_ref, block, table, rows, masks, store):
    half, y0, y7, z0, z7 = masks

    def near(ox, oy, oz, p):
        slot = nb_ref[block, 9 * ox + 3 * oy + oz]
        return table[slot, rows, p * LANES : (p + 1) * LANES]

    def sides(lo, mid, hi, first, last, step):
        before = jnp.where(first, rolled(lo, -7 * step), rolled(mid, step))
        after = jnp.where(last, rolled(hi, 7 * step), rolled(mid, -step))
        return before, mid, after

    for a in range(3):
        for p in range(PIECES):
            plane = []
            for oy in range(3):
                line = []
                for oz in range(3):
                    here = near(1, oy, oz, p)
                    if a == 0:
                        other = near(1, oy, oz, p - 1) if p > 0 else near(0, oy, oz, PIECES - 1)
                        here = rolled(jnp.where(half, here, other), 64)
                    elif a == 2:
                        other = near(1, oy, oz, p + 1) if p < PIECES - 1 else near(2, oy, oz, 0)
                        here = rolled(jnp.where(half, other, here), 64)
                    line.append(here)
                plane.append(line)
            by_z = [sides(plane[0][oz], plane[1][oz], plane[2][oz], y0, y7, 8) for oz in range(3)]
            for b in range(3):
                cells = sides(by_z[0][b], by_z[1][b], by_z[2][b], z0, z7, 1)
                for c in range(3):
                    store(9 * a + 3 * b + c, p, cells[c])


def scatter_patch(nb_ref, block, grads, parts, table_grad, rows, masks, load):
    half, y0, y7, z0, z7 = masks

    def sides(before, mid, after, first, last, step):
        zero = jnp.zeros_like(mid)
        lo = jnp.where(last, rolled(before, 7 * step), zero)
        hi = jnp.where(first, rolled(after, -7 * step), zero)
        mid = mid + jnp.where(last, zero, rolled(before, -step))
        mid = mid + jnp.where(first, zero, rolled(after, step))
        return lo, mid, hi

    for a in range(3):
        for p in range(PIECES):
            by_y = [
                sides(*[load(9 * a + 3 * b + c, p) for c in range(3)], z0, z7, 1) for b in range(3)
            ]
            for oz in range(3):
                folded = sides(by_y[0][oz], by_y[1][oz], by_y[2][oz], y0, y7, 8)
                for oy in range(3):
                    value = folded[oy]
                    if a != 1:
                        value = rolled(value, 64)
                    parts[a, 3 * oy + oz, :, p * LANES : (p + 1) * LANES] = value

    def part(a, j, p):
        return parts[a, j, :, p * LANES : (p + 1) * LANES]

    def add(slot, p, value):
        at = (slot, rows, slice(p * LANES, (p + 1) * LANES))
        table_grad[at] = table_grad[at] + value

    for j in range(9):
        zero = jnp.zeros((CH, LANES), F32)
        slot = nb_ref[block, 9 + j]
        pieces = []
        for p in range(PIECES):
            low = part(0, j, p)
            if p > 0:
                low = low + part(2, j, p - 1)
            high = part(2, j, p)
            if p < PIECES - 1:
                high = high + part(0, j, p + 1)
            pieces.append(part(1, j, p) + jnp.where(half, low, high))
        whole = (slot, rows, slice(None))
        table_grad[whole] = table_grad[whole] + jnp.concatenate(pieces, axis=1)
        add(nb_ref[block, j], PIECES - 1, jnp.where(half, zero, part(0, j, 0)))
        add(nb_ref[block, 18 + j], 0, jnp.where(half, part(2, j, PIECES - 1), zero))


def level_kernel(
    scale,
    nb_ref,
    live_ref,
    table_hbm,
    cot_ref,
    w_ref,
    wt_ref,
    lift_ref,
    liftt_ref,
    drop_ref,
    dropt_ref,
    out_ref,
    tg_ref,
    wg_ref,
    table,
    cols_hi,
    cols_lo,
    dcols,
    parts,
    wsplit,
    wtsplit,
    acc,
    grad3,
    sem,
):
    slots = table_hbm.shape[0]
    count, chans = cot_ref.shape[:2]
    fetch = pltpu.make_async_copy(table_hbm, table.at[pl.ds(0, slots)], sem)
    fetch.start()
    table[slots] = jnp.zeros((chans, VOX), F32)
    tg_ref[...] = jnp.zeros_like(tg_ref)
    acc[...] = jnp.zeros_like(acc)
    w_hi, w_lo = split(w_ref[...])
    wsplit[:chans] = w_hi
    wsplit[chans:] = w_lo
    wt_hi, wt_lo = split(wt_ref[...])
    wtsplit[...] = jnp.concatenate(
        [wt_hi.astype(F32), wt_lo.astype(F32), wt_hi.astype(F32)], axis=1
    ).astype(BF16)

    lane = lax.broadcasted_iota(jnp.int32, (CH, LANES), 1)
    y, z = (lane // 8) % 8, lane % 8
    masks = (lane < 64, y == 0, y == 7, z == 0, z == 7)

    def spot(v):
        return (v // 128) * 16 + ((v // 16) % 4) * 4 + (v % 8) // 2

    pool = (
        spot(lax.broadcasted_iota(jnp.int32, (VOX, 64), 0))
        == lax.broadcasted_iota(jnp.int32, (VOX, 64), 1)
    ).astype(F32).astype(BF16)
    spread = (
        lax.broadcasted_iota(jnp.int32, (64, VOX), 0)
        == spot(lax.broadcasted_iota(jnp.int32, (64, VOX), 1))
    ).astype(F32).astype(BF16)

    def times(x, m):
        hi, lo = split(x)
        return dot(hi, m) + dot(lo, m)

    def exact(a, b):
        return jnp.dot(a, b, preferred_element_type=F32, precision=HIGH)

    fetch.wait()

    def one_block(b, _):
        def build(c, _):
            rows = pl.ds(pl.multiple_of(c * CH, CH), CH)

            def store(k, p, value):
                hi, lo = split(value)
                at = (pl.ds(pl.multiple_of(k * chans + c * CH, CH), CH), slice(p * LANES, (p + 1) * LANES))
                cols_hi[at] = hi
                cols_lo[at] = lo

            gather_patch(nb_ref, b, table, rows, masks, store)
            return 0

        lax.fori_loop(0, chans // CH, build, 0)
        both = dot(wsplit[...], cols_hi[...])
        pre = both[:chans] + both[chans:] + dot(wsplit[:chans], cols_lo[...])
        live = live_ref[b]
        sig = 1.0 / (1.0 + jnp.exp(-pre))
        hidden = pre * sig
        pooled = times(hidden * live, pool) * 0.125
        lifted_pre = exact(lift_ref[...], pooled)
        lift_sig = 1.0 / (1.0 + jnp.exp(-lifted_pre))
        coarse = exact(drop_ref[...], lifted_pre * lift_sig)
        out_ref[b] = live * (hidden + times(coarse, spread))
        out_grad = live * cot_ref[b]
        coarse_grad = times(out_grad, pool)
        lifted_grad = exact(dropt_ref[...], coarse_grad)
        lifted_pre_grad = lifted_grad * lift_sig * (1.0 + lifted_pre * (1.0 - lift_sig))
        pooled_grad = exact(liftt_ref[...], lifted_pre_grad)
        hidden_grad = out_grad + live * times(pooled_grad, spread) * 0.125
        pre_grad = hidden_grad * sig * (1.0 + pre * (1.0 - sig))
        g_hi, g_lo = split(pre_grad)
        grad3[:chans] = g_hi
        grad3[chans : 2 * chans] = g_hi
        grad3[2 * chans :] = g_lo
        both = dot_nt(grad3[chans:], cols_hi[...])
        acc[...] += both[:chans] + both[chans:] + dot_nt(grad3[:chans], cols_lo[...])

        def fold(c, _):
            rows = pl.ds(pl.multiple_of(c * CH, CH), CH)
            own = pl.ds(pl.multiple_of(c * (K * CH), CH), K * CH)
            dcols[...] = dot(wtsplit[own], grad3[...])

            def load(k, p):
                return dcols[k * CH : (k + 1) * CH, p * LANES : (p + 1) * LANES]

            scatter_patch(nb_ref, b, dcols, parts, tg_ref, rows, masks, load)
            return 0

        lax.fori_loop(0, chans // CH, fold, 0)
        return 0

    lax.fori_loop(0, count, one_block, 0)
    for k in range(K):
        wg_ref[k] = acc[:, k * chans : (k + 1) * chans] * scale


def level(nb, live, table, cot, weight, lift, drop, scale):
    count, chans = cot.shape[:2]
    slots = table.shape[0]
    w = weight.transpose(1, 0, 2).reshape(chans, K * chans)
    wt = weight.reshape(K, chans, chans // CH, CH).transpose(2, 0, 3, 1).reshape(K * chans, chans)
    smem = pl.BlockSpec(memory_space=pltpu.SMEM)
    vmem = pl.BlockSpec(memory_space=pltpu.VMEM)
    return pl.pallas_call(
        functools.partial(level_kernel, scale),
        out_shape=(
            jax.ShapeDtypeStruct((count, chans, VOX), F32),
            jax.ShapeDtypeStruct((slots + 1, chans, VOX), F32),
            jax.ShapeDtypeStruct((K, chans, chans), F32),
        ),
        in_specs=[smem, smem, pl.BlockSpec(memory_space=pl.ANY)] + [vmem] * 7,
        out_specs=(vmem, vmem, vmem),
        scratch_shapes=[
            pltpu.VMEM((slots + 1, chans, VOX), F32),
            pltpu.VMEM((K * chans, VOX), BF16),
            pltpu.VMEM((K * chans, VOX), BF16),
            pltpu.VMEM((K * CH, VOX), F32),
            pltpu.VMEM((3, 9, CH, VOX), F32),
            pltpu.VMEM((2 * chans, K * chans), BF16),
            pltpu.VMEM((K * chans, 3 * chans), BF16),
            pltpu.VMEM((chans, K * chans), F32),
            pltpu.VMEM((3 * chans, VOX), BF16),
            pltpu.SemaphoreType.DMA,
        ],
        compiler_params=pltpu.CompilerParams(vmem_limit_bytes=48 * 1024 * 1024),
        name="level",
    )(nb, live, table, cot, w, wt, lift, lift.T, drop, drop.T)


def shifted(array, by):
    length = lax.axis_size("slab")
    pairs = [(i, i + by) for i in range(length) if 0 <= i + by < length]
    return lax.ppermute(array, "slab", pairs)


def shards(features, block_count, neighbours, conv_weight, lift_weight, drop_weight, cotangent):
    blocks = features.shape[0]
    subs = lax.axis_size("sub")
    count = blocks // subs
    first = lax.axis_index("sub") * count
    narrow = jnp.concatenate([shifted(features, 1), features, shifted(features, -1)], axis=0)
    table = lax.all_gather(narrow, "sub", axis=1, tiled=True)
    cot = lax.all_to_all(cotangent, "sub", 0, 1, tiled=True)
    weight = lax.all_gather(conv_weight, "sub", axis=1, tiled=True)
    drop = lax.all_gather(drop_weight, "sub", axis=0, tiled=True)
    nb = lax.dynamic_slice_in_dim(neighbours, first, count, 0)
    live = (first + lax.iota(jnp.int32, count) < block_count[0]).astype(F32)
    scale = float((VOX * blocks * lax.axis_size("slab")) ** -0.5)
    out, table_grad, weight_part = level(nb, live, table, cot, weight, lift_weight, drop, scale)
    output = lax.all_to_all(out, "sub", 1, 0, tiled=True)
    mine = lax.psum_scatter(table_grad[: 3 * blocks], "sub", scatter_dimension=1, tiled=True)
    feature_grad = (
        mine[blocks : 2 * blocks]
        + shifted(mine[:blocks], -1)
        + shifted(mine[2 * blocks :], 1)
    )
    own = lax.psum_scatter(weight_part, "sub", scatter_dimension=1, tiled=True)
    weight_grad = lax.psum(own, "slab")
    return (output, feature_grad, weight_grad)


def solution(mesh):
    return jax.shard_map(
        shards,
        mesh=mesh,
        in_specs=(
            P(("groups", "slab"), "sub", None),
            P(("groups", "slab")),
            P(("groups", "slab"), None),
            P(None, "sub", None),
            P(),
            P("sub", None),
            P(("groups", "slab"), "sub", None),
        ),
        out_specs=(
            P(("groups", "slab"), "sub", None),
            P(("groups", "slab"), "sub", None),
            P(None, ("groups", "sub"), None),
        ),
        check_vma=False,
    )
```

```python
import functools

import jax
import jax.numpy as jnp
from jax import lax
from jax.experimental import pallas as pl
from jax.experimental.pallas import tpu as pltpu
from jax.sharding import PartitionSpec as P

HIGH = lax.Precision.HIGHEST
F32 = jnp.float32
BF16 = jnp.bfloat16
K = 27
VOX = 512
LANES = 128
CH = 16
PIECES = VOX // LANES


def split(x):
    hi = x.astype(BF16)
    lo = (x - hi.astype(F32)).astype(BF16)
    return hi, lo


def dot(a, b):
    return jnp.dot(a, b, preferred_element_type=F32)


def dot_nt(a, b):
    return lax.dot_general(a, b, (((1,), (1,)), ((), ())), preferred_element_type=F32)


def rolled(x, by):
    return pltpu.roll(x, by % LANES, axis=1)


def gather_patch(nb_ref, block, table, rows, masks, store):
    half, y0, y7, z0, z7 = masks

    def near(ox, oy, oz, p):
        slot = nb_ref[block, 9 * ox + 3 * oy + oz]
        return table[slot, rows, p * LANES : (p + 1) * LANES]

    def sides(lo, mid, hi, first, last, step):
        before = jnp.where(first, rolled(lo, -7 * step), rolled(mid, step))
        after = jnp.where(last, rolled(hi, 7 * step), rolled(mid, -step))
        return before, mid, after

    for a in range(3):
        for p in range(PIECES):
            plane = []
            for oy in range(3):
                line = []
                for oz in range(3):
                    here = near(1, oy, oz, p)
                    if a == 0:
                        other = near(1, oy, oz, p - 1) if p > 0 else near(0, oy, oz, PIECES - 1)
                        here = rolled(jnp.where(half, here, other), 64)
                    elif a == 2:
                        other = near(1, oy, oz, p + 1) if p < PIECES - 1 else near(2, oy, oz, 0)
                        here = rolled(jnp.where(half, other, here), 64)
                    line.append(here)
                plane.append(line)
            by_z = [sides(plane[0][oz], plane[1][oz], plane[2][oz], y0, y7, 8) for oz in range(3)]
            for b in range(3):
                cells = sides(by_z[0][b], by_z[1][b], by_z[2][b], z0, z7, 1)
                for c in range(3):
                    store(9 * a + 3 * b + c, p, cells[c])


def scatter_patch(nb_ref, block, grads, parts, table_grad, rows, masks, load):
    half, y0, y7, z0, z7 = masks

    def sides(before, mid, after, first, last, step):
        zero = jnp.zeros_like(mid)
        lo = jnp.where(last, rolled(before, 7 * step), zero)
        hi = jnp.where(first, rolled(after, -7 * step), zero)
        mid = mid + jnp.where(last, zero, rolled(before, -step))
        mid = mid + jnp.where(first, zero, rolled(after, step))
        return lo, mid, hi

    for a in range(3):
        for p in range(PIECES):
            by_y = [
                sides(*[load(9 * a + 3 * b + c, p) for c in range(3)], z0, z7, 1) for b in range(3)
            ]
            for oz in range(3):
                folded = sides(by_y[0][oz], by_y[1][oz], by_y[2][oz], y0, y7, 8)
                for oy in range(3):
                    value = folded[oy]
                    if a != 1:
                        value = rolled(value, 64)
                    parts[a, 3 * oy + oz, :, p * LANES : (p + 1) * LANES] = value

    def part(a, j, p):
        return parts[a, j, :, p * LANES : (p + 1) * LANES]

    def add(slot, p, value):
        at = (slot, rows, slice(p * LANES, (p + 1) * LANES))
        table_grad[at] = table_grad[at] + value

    for j in range(9):
        zero = jnp.zeros((CH, LANES), F32)
        slot = nb_ref[block, 9 + j]
        pieces = []
        for p in range(PIECES):
            low = part(0, j, p)
            if p > 0:
                low = low + part(2, j, p - 1)
            high = part(2, j, p)
            if p < PIECES - 1:
                high = high + part(0, j, p + 1)
            pieces.append(part(1, j, p) + jnp.where(half, low, high))
        whole = (slot, rows, slice(None))
        table_grad[whole] = table_grad[whole] + jnp.concatenate(pieces, axis=1)
        add(nb_ref[block, j], PIECES - 1, jnp.where(half, zero, part(0, j, 0)))
        add(nb_ref[block, 18 + j], 0, jnp.where(half, part(2, j, PIECES - 1), zero))


def lane_masks():
    lane = lax.broadcasted_iota(jnp.int32, (CH, LANES), 1)
    y, z = (lane // 8) % 8, lane % 8
    return lane < 64, y == 0, y == 7, z == 0, z == 7


def forward_kernel(
    scale,
    nb_ref,
    live_ref,
    below_ref,
    below_x_ref,
    own_ref,
    own_x_ref,
    above_ref,
    above_x_ref,
    cot_ref,
    cot_x_ref,
    w_ref,
    lift_ref,
    liftt_ref,
    drop_ref,
    dropt_ref,
    out_ref,
    out_x_ref,
    grad_ref,
    wg_ref,
    wg_x_ref,
    table,
    cols_hi,
    cols_lo,
    wsplit,
    acc,
):
    count, half = cot_ref.shape[:2]
    chans = 2 * half
    blocks = own_ref.shape[0]
    sources = ((below_ref, below_x_ref), (own_ref, own_x_ref), (above_ref, above_x_ref))
    for i, (first, second) in enumerate(sources):
        table[i * blocks : (i + 1) * blocks, :half] = first[...]
        table[i * blocks : (i + 1) * blocks, half:] = second[...]
    table[3 * blocks] = jnp.zeros((chans, VOX), F32)
    acc[...] = jnp.zeros_like(acc)
    w_hi, w_lo = split(w_ref[...])
    wsplit[:chans] = w_hi
    wsplit[chans:] = w_lo
    masks = lane_masks()

    def spot(v):
        return (v // 128) * 16 + ((v // 16) % 4) * 4 + (v % 8) // 2

    pool = (
        spot(lax.broadcasted_iota(jnp.int32, (VOX, 64), 0))
        == lax.broadcasted_iota(jnp.int32, (VOX, 64), 1)
    ).astype(F32).astype(BF16)
    spread = (
        lax.broadcasted_iota(jnp.int32, (64, VOX), 0)
        == spot(lax.broadcasted_iota(jnp.int32, (64, VOX), 1))
    ).astype(F32).astype(BF16)

    def times(x, m):
        hi, lo = split(x)
        return dot(hi, m) + dot(lo, m)

    def exact(a, b):
        return jnp.dot(a, b, preferred_element_type=F32, precision=HIGH)

    def one_block(b, _):
        def build(c, _):
            rows = pl.ds(pl.multiple_of(c * CH, CH), CH)

            def store(k, p, value):
                hi, lo = split(value)
                at = (
                    pl.ds(pl.multiple_of(k * chans + c * CH, CH), CH),
                    slice(p * LANES, (p + 1) * LANES),
                )
                cols_hi[at] = hi
                cols_lo[at] = lo

            gather_patch(nb_ref, b, table, rows, masks, store)
            return 0

        lax.fori_loop(0, chans // CH, build, 0)
        both = dot(wsplit[...], cols_hi[...])
        pre = both[:chans] + both[chans:] + dot(wsplit[:chans], cols_lo[...])
        live = live_ref[b]
        sig = 1.0 / (1.0 + jnp.exp(-pre))
        hidden = pre * sig
        pooled = times(hidden * live, pool) * 0.125
        lifted_pre = exact(lift_ref[...], pooled)
        lift_sig = 1.0 / (1.0 + jnp.exp(-lifted_pre))
        coarse = exact(drop_ref[...], lifted_pre * lift_sig)
        out = live * (hidden + times(coarse, spread))
        out_ref[b] = out[:half]
        out_x_ref[b] = out[half:]
        out_grad = live * jnp.concatenate([cot_ref[b], cot_x_ref[b]], axis=0)
        coarse_grad = times(out_grad, pool)
        lifted_grad = exact(dropt_ref[...], coarse_grad)
        lifted_pre_grad = lifted_grad * lift_sig * (1.0 + lifted_pre * (1.0 - lift_sig))
        pooled_grad = exact(liftt_ref[...], lifted_pre_grad)
        hidden_grad = out_grad + live * times(pooled_grad, spread) * 0.125
        pre_grad = hidden_grad * sig * (1.0 + pre * (1.0 - sig))
        g_hi, g_lo = split(pre_grad)
        g_both = jnp.concatenate([g_hi, g_lo], axis=0)
        grad_ref[b] = jnp.concatenate([g_hi, g_both], axis=0)
        both = dot_nt(g_both, cols_hi[...])
        acc[...] += both[:chans] + both[chans:] + dot_nt(g_hi, cols_lo[...])
        return 0

    lax.fori_loop(0, count, one_block, 0)
    for k in range(K):
        wg_ref[k] = acc[:half, k * chans : (k + 1) * chans] * scale
        wg_x_ref[k] = acc[half:, k * chans : (k + 1) * chans] * scale


def backward_kernel(nb_ref, grad_ref, wt_ref, tg_ref, tg_x_ref, total, dcols, parts, wtsplit):
    count = grad_ref.shape[0]
    slots, half = tg_ref.shape[:2]
    chans = 2 * half
    total[...] = jnp.zeros_like(total)
    wt_hi, wt_lo = split(wt_ref[...])
    wtsplit[...] = jnp.concatenate(
        [wt_hi.astype(F32), wt_lo.astype(F32), wt_hi.astype(F32)], axis=1
    ).astype(BF16)
    masks = lane_masks()

    def one_block(b, _):
        def fold(c, _):
            rows = pl.ds(pl.multiple_of(c * CH, CH), CH)
            own = pl.ds(pl.multiple_of(c * (K * CH), CH), K * CH)
            dcols[...] = dot(wtsplit[own], grad_ref[b])

            def load(k, p):
                return dcols[k * CH : (k + 1) * CH, p * LANES : (p + 1) * LANES]

            scatter_patch(nb_ref, b, dcols, parts, total, rows, masks, load)
            return 0

        lax.fori_loop(0, chans // CH, fold, 0)
        return 0

    lax.fori_loop(0, count, one_block, 0)
    tg_ref[...] = total[:slots, :half]
    tg_x_ref[...] = total[:slots, half:]


SMEM = pl.BlockSpec(memory_space=pltpu.SMEM)
VMEM = pl.BlockSpec(memory_space=pltpu.VMEM)


def params(mib):
    return pltpu.CompilerParams(vmem_limit_bytes=mib * 1024 * 1024)


def cost(us):
    return pl.CostEstimate(flops=us * 10**9, bytes_accessed=us * 3 * 10**6, transcendentals=0)


def level_forward(nb, live, table, cot, weight, lift, drop, scale):
    count, half = cot[0].shape[:2]
    chans = 2 * half
    slots = 3 * table[0].shape[0]
    w = weight.transpose(1, 0, 2).reshape(chans, K * chans)
    part = jax.ShapeDtypeStruct((count, half, VOX), F32)
    weight_part = jax.ShapeDtypeStruct((K, half, chans), F32)
    return pl.pallas_call(
        functools.partial(forward_kernel, scale),
        out_shape=(
            part,
            part,
            jax.ShapeDtypeStruct((count, 3 * chans, VOX), BF16),
            weight_part,
            weight_part,
        ),
        in_specs=[SMEM, SMEM] + [VMEM] * 13,
        out_specs=(VMEM,) * 5,
        scratch_shapes=[
            pltpu.VMEM((slots + 1, chans, VOX), F32),
            pltpu.VMEM((K * chans, VOX), BF16),
            pltpu.VMEM((K * chans, VOX), BF16),
            pltpu.VMEM((2 * chans, K * chans), BF16),
            pltpu.VMEM((chans, K * chans), F32),
        ],
        compiler_params=params(40),
        cost_estimate=cost(35),
        name="level_forward",
    )(nb, live, *table, *cot, w, lift, lift.T, drop, drop.T)


def level_backward(nb, grad, weight, slots):
    chans = weight.shape[1]
    half = chans // 2
    wt = weight.reshape(K, chans, chans // CH, CH).transpose(2, 0, 3, 1).reshape(K * chans, chans)
    part = jax.ShapeDtypeStruct((slots, half, VOX), F32)
    return pl.pallas_call(
        backward_kernel,
        out_shape=(part, part),
        in_specs=[SMEM, VMEM, VMEM],
        out_specs=(VMEM, VMEM),
        scratch_shapes=[
            pltpu.VMEM((slots + 1, chans, VOX), F32),
            pltpu.VMEM((K * CH, VOX), F32),
            pltpu.VMEM((3, 9, CH, VOX), F32),
            pltpu.VMEM((K * chans, 3 * chans), BF16),
        ],
        compiler_params=params(40),
        cost_estimate=cost(30),
        name="level_backward",
    )(nb, grad, wt)


def shifted(array, by):
    length = lax.axis_size("slab")
    pairs = [(i, i + by) for i in range(length) if 0 <= i + by < length]
    return lax.ppermute(array, "slab", pairs)


def swap(array):
    return lax.ppermute(array, "sub", [(0, 1), (1, 0)])


def slab_sum(array):
    length = lax.axis_size("slab")
    if length & (length - 1):
        return lax.psum(array, "slab")
    step = 1
    while step < length:
        array = array + lax.ppermute(array, "slab", [(i, i ^ step) for i in range(length)])
        step *= 2
    return array


def shards(features, block_count, neighbours, conv_weight, lift_weight, drop_weight, cotangent):
    blocks, half = features.shape[:2]
    sub = lax.axis_index("sub")
    lead = sub == 0
    count = blocks // 2
    first = sub * count

    def own_first(array, axis):
        return jnp.where(lead, array, jnp.roll(array, half, axis=axis))

    below, above = shifted(features, 1), shifted(features, -1)
    table = (below, swap(below), features, swap(features), above, swap(above))
    cot = (
        lax.dynamic_slice_in_dim(cotangent, first, count, 0),
        swap(lax.dynamic_slice_in_dim(cotangent, count - first, count, 0)),
    )
    weight = own_first(jnp.concatenate([conv_weight, swap(conv_weight)], axis=1), 2)
    drop = jnp.concatenate([drop_weight, swap(drop_weight)], axis=0)
    nb = lax.dynamic_slice_in_dim(neighbours, first, count, 0)
    live = (first + lax.iota(jnp.int32, count) < block_count[0]).astype(F32)
    scale = float((VOX * blocks * lax.axis_size("slab")) ** -0.5)
    out, out_x, grad, part, part_x = level_forward(
        nb, live, table, cot, weight, own_first(lift_weight, 1), drop, scale
    )
    table_grad, table_grad_x = level_backward(nb, grad, weight, 3 * blocks)
    received = swap(out_x)
    output = jnp.concatenate(
        [jnp.where(lead, out, received), jnp.where(lead, received, out)], axis=0
    )
    weight_grad = slab_sum(own_first(part, 2) + swap(own_first(part_x, 2)))
    mine = table_grad + swap(table_grad_x)
    feature_grad = (
        mine[blocks : 2 * blocks]
        + shifted(mine[:blocks], -1)
        + shifted(mine[2 * blocks :], 1)
    )
    return (output, feature_grad, weight_grad)


def solution(mesh):
    return jax.shard_map(
        shards,
        mesh=mesh,
        in_specs=(
            P(("groups", "slab"), "sub", None),
            P(("groups", "slab")),
            P(("groups", "slab"), None),
            P(None, "sub", None),
            P(),
            P("sub", None),
            P(("groups", "slab"), "sub", None),
        ),
        out_specs=(
            P(("groups", "slab"), "sub", None),
            P(("groups", "slab"), "sub", None),
            P(None, ("groups", "sub"), None),
        ),
        check_vma=False,
    )
```
